32 devices in a mesh: src: 4 (over x, core), rows: 8 (over z, y).
Axes of the slice: x: 2, y: 2, z: 4, core: 2. Of those that a mesh axis runs over, the one named last changes fastest.
Arguments:
- mask_param: float32 [128, 8192], P('rows'), may hold values from -6 to 6
- target: int32 [128, 8192], P('rows', 'src'), may hold values 0 or 1
- source_weight: float32 [4], replicated, may hold values from 0.25 to 4
- row_shift: int32 [4], replicated, may hold values from -2 to 2
- col_shift: int32 [4], replicated, may hold values from -32 to 32
Outputs:
- mask_grad: float32 [128, 8192], P('rows', 'src')
The draws below stay inside these ranges and needn't reach their ends.
All inputs are finite; a program needn't handle non-finite values. No bound on the sum of `target` on one device may be relied on, other than what follows from the above.
Results may differ from the reference program's by a relative error of at most 0.0003.
Values sent between devices are 32-bit elements; how exact they have to be, the bound alone decides.
A program may use at most 64 MiB of HBM per device.

```python
import math
import jax
import jax.numpy as jnp
from jax import lax

NC = 8192
NR = 128
SRC = 4
KR = 8
KC = 128


def touch_ends(result, key, least, high):
    longest = result.shape.index(max(result.shape))
    spots = []
    for shift in (0, 1):
        where = [jax.random.randint(jax.random.fold_in(key, axis), (), 0, length) for axis, length in enumerate(result.shape)]
        where[longest] = (where[longest] + shift) % result.shape[longest]
        spots.append(tuple(where))
    return result.at[spots[0]].set(least).at[spots[1]].set(high)


def shard_levels(own_key, shape, cuts, least, largest):
    level, own = 1.0, jax.random.fold_in(own_key, 6)
    for axis_at, shards_of in cuts:
        heights = jnp.exp(jax.random.uniform(jax.random.fold_in(own, axis_at), (shards_of,), jnp.float32, least / len(cuts), largest / len(cuts)))
        level = level * jnp.repeat(heights, shape[axis_at] // shards_of).reshape([-1 if axis == axis_at else 1 for axis in range(len(shape))])
    return level


def normal_values(rng, dims, scale, limit, cuts=(), kind=jnp.bfloat16):
    values = jax.random.normal(rng, dims, jnp.float32) * scale
    if len(cuts) > 0:
        values = shard_levels(rng, dims, cuts, -0.22, 0.18) * values
    return jnp.clip(values, min=-limit, max=limit).astype(kind)


def setup_inputs(seed: int = 0) -> dict:
    arg_keys = jax.random.split(jax.random.key(seed), 6)
    mask_param = normal_values(arg_keys[0], (NR, NC), 1.0, 6.0, ((0, 8),), jnp.float32)
    target = touch_ends((jax.random.randint(arg_keys[1], (NR, NC), 0, 2) < 1).astype(jnp.int32), jax.random.fold_in(arg_keys[1], 1), 0, 1)
    source_weight = jnp.clip(jnp.exp(jax.random.uniform(arg_keys[2], (SRC,), jnp.float32, math.log(0.25), math.log(4.0))), 0.25, 4.0)
    row_shift = touch_ends(jax.random.randint(arg_keys[3], (SRC,), -(KR // 4), KR // 4 + 1), jax.random.fold_in(arg_keys[3], 1), -(KR // 4), (KR // 4 + 1) - 1).astype(jnp.int32)
    col_shift = touch_ends(jax.random.randint(arg_keys[4], (SRC,), -(KC // 4), KC // 4 + 1), jax.random.fold_in(arg_keys[4], 1), -(KC // 4), (KC // 4 + 1) - 1).astype(jnp.int32)
    return dict(mask_param=mask_param, target=target, source_weight=source_weight, row_shift=row_shift, col_shift=col_shift)


steepness = 250.0
threshold_level = 0.25
loss_weight = 8.0


def centered(number):
    return jnp.arange(number, dtype=jnp.int32) - number // 2


def pupil_mask(row_offset, col_offset):
    radius_rows = KR // 4
    radius_cols = KC // 4
    row_term = (centered(KR) + row_offset) ** 2 * (radius_cols * radius_cols)
    col_term = (centered(KC) + col_offset) ** 2 * (radius_rows * radius_rows)
    limit_value = (radius_rows * radius_cols) ** 2
    return (row_term[:, None] + col_term[None, :] <= limit_value).astype(jnp.float32)


def reference(mask_param, target, source_weight, row_shift, col_shift):
    opening = jax.nn.sigmoid(mask_param)
    row_index = jnp.mod(centered(KR), NR).astype(jnp.int32)
    col_index = jnp.mod(centered(KC), NC).astype(jnp.int32)
    spectrum = jnp.fft.fft2(opening, norm="ortho")
    band_spec = spectrum[row_index][:, col_index]
    weights = source_weight / jnp.sum(source_weight)

    def spread_band(values):
        padded = jnp.zeros((NR, NC), band_spec.dtype)
        return padded.at[row_index[:, None], col_index[None, :]].set(values)

    def field_of(point_row, point_col):
        opened = band_spec * pupil_mask(point_row, point_col)
        return jnp.fft.ifft2(spread_band(opened), norm="ortho")

    def add_intensity(running, entries):
        weight, point_row, point_col = entries
        field_now = field_of(point_row, point_col)
        return running + weight * (jnp.real(field_now) ** 2 + jnp.imag(field_now) ** 2), None

    intensity = lax.scan(add_intensity, jnp.zeros((NR, NC), jnp.float32), (weights, row_shift, col_shift))[0]
    resist = jax.nn.sigmoid(steepness * (intensity - threshold_level))
    slope = 2.0 * loss_weight * (resist - target.astype(jnp.float32)) * steepness * resist * (1.0 - resist)

    def add_adjoint(running, entries):
        weight, point_row, point_col = entries
        field_now = field_of(point_row, point_col)
        cotangent = 2.0 * weight * slope * field_now
        back_band = jnp.fft.fft2(cotangent, norm="ortho")[row_index][:, col_index]
        return running + pupil_mask(point_row, point_col) * back_band, None

    adjoint = lax.scan(add_adjoint, jnp.zeros((KR, KC), band_spec.dtype), (weights, row_shift, col_shift))[0]
    grad_open = jnp.real(jnp.fft.ifft2(spread_band(adjoint), norm="ortho"))
    return (grad_open * opening * (1.0 - opening)).astype(jnp.float32)
```

```python
import functools
import math

import jax
import jax.numpy as jnp
import numpy as np
from jax import lax
from jax.experimental import pallas as pl
from jax.experimental.pallas import tpu as pltpu
from jax.sharding import PartitionSpec as P

steepness = 250.0
threshold_level = 0.25
loss_weight = 8.0
lift = 2.0**60
highest = lax.Precision.HIGHEST
MESH = pl.DeviceIdType.MESH


def product(left, right):
    return jnp.dot(left, right, precision=highest, preferred_element_type=jnp.float32)


def logistic(value):
    return 1.0 / (1.0 + jnp.exp(-value))


def phase_tables(frequency, position, period):
    angles = np.mod(np.outer(frequency, position), period) * (2.0 * math.pi / period)
    return np.cos(angles), np.sin(angles)


def make_tables(total_rows, total_cols, row_block, band_rows, band_cols):
    width = 2 * band_cols
    step = total_cols // width
    row_freq = np.arange(band_rows) - band_rows // 2
    col_freq = np.arange(band_cols) - band_cols // 2
    inside = np.arange(width)
    cos, sin = phase_tables(col_freq, inside, total_cols)
    last = np.concatenate([cos, -sin], axis=0)
    first = last.T
    cos, sin = phase_tables(col_freq, inside * step, total_cols)
    coarse = np.block([[cos, sin], [-sin, cos]])
    offset = inside[None, :] - step * inside[:, None]
    harmonics = np.arange(1, band_cols)
    angles = np.mod(offset[:, :, None] * harmonics, total_cols) * (2.0 * math.pi / total_cols)
    spread = (1.0 + 2.0 * np.cos(angles).sum(axis=2)) / width
    cos, sin = phase_tables(np.arange(total_cols // width), col_freq * width, total_cols)
    turn = np.concatenate([cos, sin], axis=1)
    cos, sin = phase_tables(row_freq, np.arange(total_rows), total_rows)
    blocks = []
    for start in range(0, total_rows, row_block):
        part = slice(start, start + row_block)
        blocks.append(np.block([[cos[:, part], sin[:, part]], [-sin[:, part], cos[:, part]]]))
    rows_in = np.concatenate(blocks, axis=0)
    rows_out = np.concatenate([block.T for block in blocks], axis=0)
    made = (first, coarse, spread, spread.T, coarse.T, last, turn, rows_in, rows_out)
    return [np.ascontiguousarray(table, dtype=np.float32) for table in made]


def kernel(
    src_count, row_count, band_rows,
    weight_ref, row_shift_ref, col_shift_ref, mask_hbm, target_hbm,
    first_hbm, coarse_hbm, spread_hbm, gather_hbm, back_hbm, last_hbm, turn_ref, rows_in_ref, rows_out_ref,
    out_ref,
    mask_ref, target_ref, first_ref, coarse_ref, spread_ref, gather_ref, back_ref, last_ref,
    send_a, send_b, send_c, recv_a, recv_b, recv_c,
    load_sem, send_sem_a, send_sem_b, send_sem_c, recv_sem_a, recv_sem_b, recv_sem_c,
):
    src_index = lax.axis_index("src")
    row_index = lax.axis_index("rows")
    row_block, total_cols = mask_ref.shape
    col_share = target_ref.shape[1]
    width = first_ref.shape[0]
    band_cols = width // 2
    points = weight_ref.shape[0]
    block_count = total_cols // width
    own_count = col_share // width
    roll_step = width * width // total_cols
    total = row_block * row_count * total_cols

    loads = [
        pltpu.make_async_copy(source, place, load_sem.at[at])
        for at, (source, place) in enumerate(
            [
                (mask_hbm, mask_ref), (first_hbm, first_ref), (coarse_hbm, coarse_ref), (spread_hbm, spread_ref),
                (target_hbm, target_ref), (gather_hbm, gather_ref), (back_hbm, back_ref), (last_hbm, last_ref),
            ]
        )
    ]
    for load in loads:
        load.start()

    def row_peer(shift):
        return {"src": src_index, "rows": lax.rem(row_index + shift, row_count)}

    def src_peer(shift):
        return {"src": lax.rem(src_index + shift, src_count), "rows": row_index}

    barrier = pltpu.get_barrier_semaphore()
    for shift in range(1, row_count):
        pl.semaphore_signal(barrier, inc=1, device_id=row_peer(shift), device_id_type=MESH)
    for shift in range(1, src_count):
        pl.semaphore_signal(barrier, inc=1, device_id=src_peer(shift), device_id_type=MESH)

    def summed(value, send, recv, send_sem, recv_sem, peer, count):
        send[...] = value
        copies = [
            pltpu.make_async_remote_copy(
                src_ref=send, dst_ref=recv.at[shift - 1],
                send_sem=send_sem.at[shift - 1], recv_sem=recv_sem.at[shift - 1],
                device_id=peer(shift), device_id_type=MESH,
            )
            for shift in range(1, count)
        ]
        for copy in copies:
            copy.start()
        for at, copy in enumerate(copies):
            copy.wait_recv()
            value = value + recv[at]
        return value, copies

    rows_in = rows_in_ref[pl.ds(pl.multiple_of(row_index * (2 * band_rows), 2 * band_rows), 2 * band_rows), :]
    rows_out = rows_out_ref[pl.ds(pl.multiple_of(row_index * (2 * row_block), 2 * row_block), 2 * row_block), :]

    def turns(block):
        return turn_ref[block : block + 1, :band_cols], turn_ref[block : block + 1, band_cols:]

    loads[0].wait()
    loads[1].wait()
    stacked = jnp.concatenate(
        [logistic(mask_ref[:, block * width : (block + 1) * width]) for block in range(block_count)], axis=0
    )
    columns = product(stacked, first_ref[...])
    col_real = columns[:row_block, :band_cols]
    col_imag = columns[:row_block, band_cols:]
    for block in range(1, block_count):
        part = columns[block * row_block : (block + 1) * row_block]
        real, imag = part[:, :band_cols], part[:, band_cols:]
        turn_cos, turn_sin = turns(block)
        col_real += real * turn_cos + imag * turn_sin
        col_imag += imag * turn_cos - real * turn_sin
    band_part = product(rows_in, jnp.concatenate([col_real, col_imag], axis=0)) * (1.0 / total)

    pl.semaphore_wait(barrier, row_count + src_count - 2)
    band, sent_a = summed(band_part, send_a, recv_a, send_sem_a, recv_sem_a, row_peer, row_count)

    own_turn = turn_ref[pl.ds(src_index * own_count, 1), :]
    own_cos, own_sin = own_turn[:, :band_cols], own_turn[:, band_cols:]
    band_real, band_imag = band[:band_rows], band[band_rows:]
    here_real = band_real * own_cos - band_imag * own_sin
    here_imag = band_real * own_sin + band_imag * own_cos

    radius_rows, radius_cols = band_rows // 4, band_cols // 4
    row_freq = lax.broadcasted_iota(jnp.int32, (band_rows, band_cols), 0) - band_rows // 2
    col_freq = lax.broadcasted_iota(jnp.int32, (band_rows, band_cols), 1) - band_cols // 2
    limit = (radius_rows * radius_cols) ** 2
    pupils = []
    for point in range(points):
        row_term = (row_freq + row_shift_ref[point]) ** 2 * (radius_cols * radius_cols)
        col_term = (col_freq + col_shift_ref[point]) ** 2 * (radius_rows * radius_rows)
        pupils.append(jnp.where(row_term + col_term <= limit, 1.0, 0.0).astype(jnp.float32))
    weights = [jnp.full((1, width), weight_ref[point], jnp.float32) for point in range(points)]
    weight_sum = functools.reduce(lambda left, right: left + right, weights)
    weights = [weight / weight_sum for weight in weights]

    opened = jnp.concatenate(
        [jnp.concatenate([pupil * here_real, pupil * here_imag], axis=0) for pupil in pupils], axis=1
    )
    heads = product(rows_out, opened)
    heads = jnp.concatenate(
        [
            jnp.concatenate(
                [
                    heads[:row_block, point * band_cols : (point + 1) * band_cols],
                    heads[row_block:, point * band_cols : (point + 1) * band_cols],
                ],
                axis=1,
            )
            for point in range(points)
        ],
        axis=0,
    )
    loads[2].wait()
    fields = product(heads, coarse_ref[...])
    field_list = [
        (
            fields[point * row_block : (point + 1) * row_block, :width],
            fields[point * row_block : (point + 1) * row_block, width:],
        )
        for point in range(points)
    ]
    excess = jnp.full((row_block, width), -threshold_level, jnp.float32)
    for weight, (real, imag) in zip(weights, field_list):
        excess += weight * (real * real + imag * imag)

    rolled = jnp.concatenate(
        [excess]
        + [pltpu.roll(excess, (width - block * roll_step) % width, 1) for block in range(1, own_count)],
        axis=0,
    )
    loads[3].wait()
    resist = logistic(steepness * product(rolled, spread_ref[...]))
    loads[4].wait()
    target = jnp.concatenate(
        [target_ref[:, block * width : (block + 1) * width] for block in range(own_count)], axis=0
    ).astype(jnp.float32)
    slope = (2.0 * loss_weight * lift) * (resist - target) * steepness * resist * (1.0 - resist)
    loads[5].wait()
    gathered = product(slope, gather_ref[...])
    low = gathered[:row_block]
    for block in range(1, own_count):
        low += pltpu.roll(gathered[block * row_block : (block + 1) * row_block], block * roll_step, 1)
    cotangents = jnp.concatenate(
        [
            jnp.concatenate([low * weight * real, low * weight * imag], axis=1)
            for weight, (real, imag) in zip(weights, field_list)
        ],
        axis=0,
    )
    loads[6].wait()
    returned = product(cotangents, back_ref[...])
    returned = jnp.concatenate(
        [
            jnp.concatenate(
                [
                    returned[point * row_block : (point + 1) * row_block, :band_cols],
                    returned[point * row_block : (point + 1) * row_block, band_cols:],
                ],
                axis=0,
            )
            for point in range(points)
        ],
        axis=1,
    )
    returned = product(rows_in, returned)
    part_real = jnp.zeros((band_rows, band_cols), jnp.float32)
    part_imag = jnp.zeros((band_rows, band_cols), jnp.float32)
    for point, pupil in enumerate(pupils):
        piece = returned[:, point * band_cols : (point + 1) * band_cols]
        part_real += pupil * piece[:band_rows]
        part_imag += pupil * piece[band_rows:]
    adjoint_part = jnp.concatenate(
        [part_real * own_cos + part_imag * own_sin, part_imag * own_cos - part_real * own_sin], axis=0
    )
    adjoint_part, sent_b = summed(adjoint_part, send_b, recv_b, send_sem_b, recv_sem_b, src_peer, src_count)
    adjoint, sent_c = summed(adjoint_part, send_c, recv_c, send_sem_c, recv_sem_c, row_peer, row_count)

    adj_real, adj_imag = adjoint[:band_rows], adjoint[band_rows:]
    adjoint = jnp.concatenate(
        [adj_real * own_cos - adj_imag * own_sin, adj_real * own_sin + adj_imag * own_cos], axis=0
    )
    head = product(rows_out, adjoint)
    head_real, head_imag = head[:row_block], head[row_block:]
    turned = []
    for block in range(own_count):
        turn_cos, turn_sin = turns(block)
        turned.append(
            jnp.concatenate(
                [head_real * turn_cos - head_imag * turn_sin, head_real * turn_sin + head_imag * turn_cos], axis=1
            )
        )
    loads[7].wait()
    grad = product(jnp.concatenate(turned, axis=0), last_ref[...])
    for block in range(own_count):
        start = pl.multiple_of(src_index * col_share + block * width, width)
        opening = logistic(mask_ref[:, pl.ds(start, width)])
        out_ref[:, block * width : (block + 1) * width] = (
            grad[block * row_block : (block + 1) * row_block] * (2.0 / (total * lift)) * opening * (1.0 - opening)
        )
    for copy in sent_a + sent_b + sent_c:
        copy.wait_send()


def local(mask_param, target, source_weight, row_shift, col_shift):
    row_block, total_cols = mask_param.shape
    src_count = lax.axis_size("src")
    row_count = lax.axis_size("rows")
    total_rows = row_block * row_count
    band_rows = total_rows // 16
    band_cols = total_cols // 64
    tables = make_tables(total_rows, total_cols, row_block, band_rows, band_cols)
    message = (2 * band_rows, band_cols)
    smem = pl.BlockSpec(memory_space=pltpu.SMEM)
    anywhere = pl.BlockSpec(memory_space=pl.ANY)
    vmem = pl.BlockSpec(memory_space=pltpu.VMEM)
    return pl.pallas_call(
        functools.partial(kernel, src_count, row_count, band_rows),
        out_shape=jax.ShapeDtypeStruct(target.shape, jnp.float32),
        in_specs=[smem] * 3 + [anywhere] * 8 + [vmem] * 3,
        out_specs=vmem,
        scratch_shapes=[
            pltpu.VMEM(mask_param.shape, jnp.float32),
            pltpu.VMEM(target.shape, jnp.int32),
        ]
        + [pltpu.VMEM(table.shape, jnp.float32) for table in tables[:6]]
        + [pltpu.VMEM(message, jnp.float32)] * 3
        + [pltpu.VMEM((count - 1,) + message, jnp.float32) for count in (row_count, src_count, row_count)]
        + [pltpu.SemaphoreType.DMA((8,))]
        + [pltpu.SemaphoreType.DMA((count - 1,)) for count in (row_count, src_count, row_count)] * 2,
        compiler_params=pltpu.CompilerParams(
            collective_id=0, has_side_effects=True, vmem_limit_bytes=60 * 1024 * 1024
        ),
    )(source_weight, row_shift, col_shift, mask_param, target, *tables)


def solution(mesh):
    placed = (P("rows", None), P("rows", "src"), P(), P(), P())
    return jax.shard_map(
        local, mesh=mesh, in_specs=placed, out_specs=P("rows", "src"), check_vma=False
    )
```

```python
import functools
import math

import jax
import jax.numpy as jnp
import numpy as np
from jax import lax
from jax.experimental import pallas as pl
from jax.experimental.pallas import tpu as pltpu
from jax.sharding import PartitionSpec as P

steepness = 250.0
threshold_level = 0.25
loss_weight = 8.0
lift = 2.0**60
highest = lax.Precision.HIGHEST
MESH = pl.DeviceIdType.MESH


def product(left, right):
    return jnp.dot(left, right, precision=highest, preferred_element_type=jnp.float32)


def logistic(value):
    return 1.0 / (1.0 + jnp.exp(-value))


def phase_tables(frequency, position, period):
    angles = np.mod(np.outer(frequency, position), period) * (2.0 * math.pi / period)
    return np.cos(angles), np.sin(angles)


def halves(value):
    high = value.astype(jnp.bfloat16)
    return high, (value - high.astype(jnp.float32)).astype(jnp.bfloat16)


def thirds(value):
    high = value.astype(jnp.bfloat16)
    rest = value - high.astype(jnp.float32)
    middle = rest.astype(jnp.bfloat16)
    return high, middle, (rest - middle.astype(jnp.float32)).astype(jnp.bfloat16)


def split_table(table_ref, parts_ref):
    parts = (halves if parts_ref.shape[0] == 2 else thirds)(table_ref[...])
    for at, part in enumerate(parts):
        parts_ref[at] = part


def full_product(left, parts_ref):
    rows = left.shape[0]
    high, middle, low = thirds(left)
    one = jnp.dot(jnp.concatenate([high, middle, low], axis=0), parts_ref[0], preferred_element_type=jnp.float32)
    two = jnp.dot(jnp.concatenate([high, middle], axis=0), parts_ref[1], preferred_element_type=jnp.float32)
    three = jnp.dot(high, parts_ref[2], preferred_element_type=jnp.float32)
    small = one[2 * rows :] + two[rows:] + three
    return one[:rows] + (one[rows : 2 * rows] + two[:rows] + small)


def split_product(left, parts_ref):
    rows = left.shape[0]
    high, low = halves(left)
    both = jnp.dot(jnp.concatenate([high, low], axis=0), parts_ref[0], preferred_element_type=jnp.float32)
    cross = jnp.dot(high, parts_ref[1], preferred_element_type=jnp.float32)
    return both[:rows] + (both[rows:] + cross)


def make_tables(total_rows, total_cols, row_block, band_rows, band_cols):
    width = 2 * band_cols
    step = total_cols // width
    row_freq = np.arange(band_rows) - band_rows // 2
    col_freq = np.arange(band_cols) - band_cols // 2
    inside = np.arange(width)
    cos, sin = phase_tables(col_freq, inside, total_cols)
    last = np.concatenate([cos, -sin], axis=0)
    first = last.T
    cos, sin = phase_tables(col_freq, inside * step, total_cols)
    coarse = np.block([[cos, sin], [-sin, cos]])
    offset = inside[None, :] - step * inside[:, None]
    harmonics = np.arange(1, band_cols)
    angles = np.mod(offset[:, :, None] * harmonics, total_cols) * (2.0 * math.pi / total_cols)
    spread = (1.0 + 2.0 * np.cos(angles).sum(axis=2)) / width
    cos, sin = phase_tables(np.arange(total_cols // width), col_freq * width, total_cols)
    turn = np.concatenate([cos, sin], axis=1)
    cos, sin = phase_tables(row_freq, np.arange(total_rows), total_rows)
    blocks = []
    for start in range(0, total_rows, row_block):
        part = slice(start, start + row_block)
        blocks.append(np.block([[cos[:, part], sin[:, part]], [-sin[:, part], cos[:, part]]]))
    rows_in = np.concatenate(blocks, axis=0)
    rows_out = np.concatenate([block.T for block in blocks], axis=0)
    made = (first, spread.T, coarse.T, last, coarse, spread, turn, rows_in, rows_out)
    return [np.ascontiguousarray(table, dtype=np.float32) for table in made]


def kernel(
    src_count, row_count, band_rows, chunks,
    weight_hbm, row_shift_hbm, col_shift_hbm, mask_hbm, target_hbm,
    first_hbm, gather_hbm, back_hbm, last_hbm, coarse_hbm, spread_hbm, turn_hbm, rows_in_hbm, rows_out_hbm,
    out_ref,
    weight_ref, row_shift_ref, col_shift_ref, mask_ref, target_ref,
    first_ref, gather_ref, back_ref, last_ref, coarse_ref, spread_ref, turn_ref, rows_in_ref, rows_out_ref,
    first_parts, gather_parts, back_parts, last_parts, coarse_parts, spread_parts,
    send_a, send_b, send_c, recv_a, recv_b, recv_c,
    load_sem, mask_sem, send_sem_a, send_sem_b, send_sem_c, recv_sem_a, recv_sem_b, recv_sem_c,
):
    src_index = lax.axis_index("src")
    row_index = lax.axis_index("rows")
    row_block, total_cols = mask_ref.shape
    col_share = target_ref.shape[1]
    width = first_ref.shape[0]
    band_cols = width // 2
    points = weight_ref.shape[0]
    block_count = total_cols // width
    own_count = col_share // width
    roll_step = width * width // total_cols
    total = row_block * row_count * total_cols

    def row_peer(shift):
        return {"src": src_index, "rows": lax.rem(row_index + shift, row_count)}

    def src_peer(shift):
        return {"src": lax.rem(src_index + shift, src_count), "rows": row_index}

    barrier = pltpu.get_barrier_semaphore()
    for shift in range(1, row_count):
        pl.semaphore_signal(barrier, inc=1, device_id=row_peer(shift), device_id_type=MESH)
    for shift in range(1, src_count):
        pl.semaphore_signal(barrier, inc=1, device_id=src_peer(shift), device_id_type=MESH)

    chunk = total_cols // chunks
    mask_loads = [
        pltpu.make_async_copy(
            mask_hbm.at[:, pl.ds(at * chunk, chunk)], mask_ref.at[:, pl.ds(at * chunk, chunk)], mask_sem.at[at]
        )
        for at in range(chunks)
    ]
    pairs = [
        (first_hbm, first_ref), (turn_hbm, turn_ref), (rows_in_hbm, rows_in_ref), (weight_hbm, weight_ref),
        (row_shift_hbm, row_shift_ref), (col_shift_hbm, col_shift_ref), (rows_out_hbm, rows_out_ref),
        (coarse_hbm, coarse_ref), (spread_hbm, spread_ref), (target_hbm, target_ref), (gather_hbm, gather_ref),
        (back_hbm, back_ref), (last_hbm, last_ref),
    ]
    loads = [pltpu.make_async_copy(source, place, load_sem.at[at]) for at, (source, place) in enumerate(pairs)]
    loads[0].start()
    for load in mask_loads + loads[1:]:
        load.start()

    def started(value, send, recv, send_sem, recv_sem, peer, count):
        send[...] = value
        copies = [
            pltpu.make_async_remote_copy(
                src_ref=send, dst_ref=recv.at[shift - 1],
                send_sem=send_sem.at[shift - 1], recv_sem=recv_sem.at[shift - 1],
                device_id=peer(shift), device_id_type=MESH,
            )
            for shift in range(1, count)
        ]
        for copy in copies:
            copy.start()
        return copies

    def summed(value, copies, recv):
        for copy in copies:
            copy.wait_recv()
        for at in range(len(copies)):
            value = value + recv[at]
        return value

    def turns(block):
        return turn_ref[block : block + 1, :band_cols], turn_ref[block : block + 1, band_cols:]

    loads[0].wait()
    split_table(first_ref, first_parts)
    stacked = []
    for at in range(chunks):
        mask_loads[at].wait()
        for start in range(at * chunk, (at + 1) * chunk, width):
            stacked.append(logistic(mask_ref[:, start : start + width]))
    for load in loads[1:3]:
        load.wait()
    columns = split_product(jnp.concatenate(stacked, axis=0), first_parts)
    rows_in = rows_in_ref[pl.ds(pl.multiple_of(row_index * (2 * band_rows), 2 * band_rows), 2 * band_rows), :]
    col_real = columns[:row_block, :band_cols]
    col_imag = columns[:row_block, band_cols:]
    for block in range(1, block_count):
        part = columns[block * row_block : (block + 1) * row_block]
        real, imag = part[:, :band_cols], part[:, band_cols:]
        turn_cos, turn_sin = turns(block)
        col_real += real * turn_cos + imag * turn_sin
        col_imag += imag * turn_cos - real * turn_sin
    band_part = product(rows_in, jnp.concatenate([col_real, col_imag], axis=0)) * (1.0 / total)

    pl.semaphore_wait(barrier, row_count + src_count - 2)
    sent_a = started(band_part, send_a, recv_a, send_sem_a, recv_sem_a, row_peer, row_count)

    for load in loads[3:]:
        load.wait()
    rows_out = rows_out_ref[pl.ds(pl.multiple_of(row_index * (2 * row_block), 2 * row_block), 2 * row_block), :]
    own_turn = turn_ref[pl.ds(src_index * own_count, 1), :]
    own_cos, own_sin = own_turn[:, :band_cols], own_turn[:, band_cols:]
    radius_rows, radius_cols = band_rows // 4, band_cols // 4
    row_freq = lax.broadcasted_iota(jnp.int32, (band_rows, band_cols), 0) - band_rows // 2
    col_freq = lax.broadcasted_iota(jnp.int32, (band_rows, band_cols), 1) - band_cols // 2
    limit = (radius_rows * radius_cols) ** 2
    pupils = []
    for point in range(points):
        row_term = (row_freq + row_shift_ref[point]) ** 2 * (radius_cols * radius_cols)
        col_term = (col_freq + col_shift_ref[point]) ** 2 * (radius_rows * radius_rows)
        pupils.append(jnp.where(row_term + col_term <= limit, 1.0, 0.0).astype(jnp.float32))
    weights = [jnp.full((1, width), weight_ref[point], jnp.float32) for point in range(points)]
    weight_sum = functools.reduce(lambda left, right: left + right, weights)
    weights = [weight / weight_sum for weight in weights]

    split_table(coarse_ref, coarse_parts)
    split_table(spread_ref, spread_parts)
    split_table(gather_ref, gather_parts)
    split_table(back_ref, back_parts)
    split_table(last_ref, last_parts)
    band = summed(band_part, sent_a, recv_a)
    band_real, band_imag = band[:band_rows], band[band_rows:]
    here_real = band_real * own_cos - band_imag * own_sin
    here_imag = band_real * own_sin + band_imag * own_cos

    opened = jnp.concatenate(
        [jnp.concatenate([pupil * here_real, pupil * here_imag], axis=0) for pupil in pupils], axis=1
    )
    heads = product(rows_out, opened)
    heads = jnp.concatenate(
        [
            jnp.concatenate(
                [
                    heads[:row_block, point * band_cols : (point + 1) * band_cols],
                    heads[row_block:, point * band_cols : (point + 1) * band_cols],
                ],
                axis=1,
            )
            for point in range(points)
        ],
        axis=0,
    )
    fields = full_product(heads, coarse_parts)
    field_list = [
        (
            fields[point * row_block : (point + 1) * row_block, :width],
            fields[point * row_block : (point + 1) * row_block, width:],
        )
        for point in range(points)
    ]
    excess = jnp.full((row_block, width), -threshold_level, jnp.float32)
    for weight, (real, imag) in zip(weights, field_list):
        excess += weight * (real * real + imag * imag)

    rolled = jnp.concatenate(
        [excess]
        + [pltpu.roll(excess, (width - block * roll_step) % width, 1) for block in range(1, own_count)],
        axis=0,
    )
    resist = logistic(steepness * full_product(rolled, spread_parts))
    target = jnp.concatenate(
        [target_ref[:, block * width : (block + 1) * width] for block in range(own_count)], axis=0
    ).astype(jnp.float32)
    slope = (2.0 * loss_weight * lift) * (resist - target) * steepness * resist * (1.0 - resist)
    gathered = split_product(slope, gather_parts)
    low = gathered[:row_block]
    for block in range(1, own_count):
        low += pltpu.roll(gathered[block * row_block : (block + 1) * row_block], block * roll_step, 1)
    cotangents = jnp.concatenate(
        [
            jnp.concatenate([low * weight * real, low * weight * imag], axis=1)
            for weight, (real, imag) in zip(weights, field_list)
        ],
        axis=0,
    )
    returned = split_product(cotangents, back_parts)
    returned = jnp.concatenate(
        [
            jnp.concatenate(
                [
                    returned[point * row_block : (point + 1) * row_block, :band_cols],
                    returned[point * row_block : (point + 1) * row_block, band_cols:],
                ],
                axis=0,
            )
            for point in range(points)
        ],
        axis=1,
    )
    returned = product(rows_in, returned)
    part_real = jnp.zeros((band_rows, band_cols), jnp.float32)
    part_imag = jnp.zeros((band_rows, band_cols), jnp.float32)
    for point, pupil in enumerate(pupils):
        piece = returned[:, point * band_cols : (point + 1) * band_cols]
        part_real += pupil * piece[:band_rows]
        part_imag += pupil * piece[band_rows:]
    adjoint_part = jnp.concatenate(
        [part_real * own_cos + part_imag * own_sin, part_imag * own_cos - part_real * own_sin], axis=0
    )
    sent_b = started(adjoint_part, send_b, recv_b, send_sem_b, recv_sem_b, src_peer, src_count)
    for block in range(own_count):
        start = pl.multiple_of(src_index * col_share + block * width, width)
        opening = logistic(mask_ref[:, pl.ds(start, width)])
        out_ref[:, block * width : (block + 1) * width] = opening * (1.0 - opening) * (2.0 / (total * lift))
    adjoint_part = summed(adjoint_part, sent_b, recv_b)
    sent_c = started(adjoint_part, send_c, recv_c, send_sem_c, recv_sem_c, row_peer, row_count)
    adjoint = summed(adjoint_part, sent_c, recv_c)

    adj_real, adj_imag = adjoint[:band_rows], adjoint[band_rows:]
    adjoint = jnp.concatenate(
        [adj_real * own_cos - adj_imag * own_sin, adj_real * own_sin + adj_imag * own_cos], axis=0
    )
    head = product(rows_out, adjoint)
    head_real, head_imag = head[:row_block], head[row_block:]
    turned = []
    for block in range(own_count):
        turn_cos, turn_sin = turns(block)
        turned.append(
            jnp.concatenate(
                [head_real * turn_cos - head_imag * turn_sin, head_real * turn_sin + head_imag * turn_cos], axis=1
            )
        )
    grad = split_product(jnp.concatenate(turned, axis=0), last_parts)
    for block in range(own_count):
        out_ref[:, block * width : (block + 1) * width] *= grad[block * row_block : (block + 1) * row_block]
    for copy in sent_a + sent_b + sent_c:
        copy.wait_send()


def local(mask_param, target, source_weight, row_shift, col_shift):
    row_block, total_cols = mask_param.shape
    src_count = lax.axis_size("src")
    row_count = lax.axis_size("rows")
    total_rows = row_block * row_count
    band_rows = total_rows // 16
    band_cols = total_cols // 64
    tables = make_tables(total_rows, total_cols, row_block, band_rows, band_cols)
    message = (2 * band_rows, band_cols)
    chunks = math.gcd(4, total_cols // (2 * band_cols))
    scalars = (source_weight, row_shift, col_shift)
    arrays = (mask_param, target, *tables)
    return pl.pallas_call(
        functools.partial(kernel, src_count, row_count, band_rows, chunks),
        out_shape=jax.ShapeDtypeStruct(target.shape, jnp.float32),
        in_specs=[pl.BlockSpec(memory_space=pl.ANY)] * (len(scalars) + len(arrays)),
        out_specs=pl.BlockSpec(memory_space=pltpu.VMEM),
        scratch_shapes=[pltpu.SMEM(array.shape, array.dtype) for array in scalars]
        + [pltpu.VMEM(array.shape, array.dtype) for array in arrays]
        + [pltpu.VMEM((2 if at < 4 else 3,) + table.shape, jnp.bfloat16) for at, table in enumerate(tables[:6])]
        + [pltpu.VMEM(message, jnp.float32)] * 3
        + [pltpu.VMEM((count - 1,) + message, jnp.float32) for count in (row_count, src_count, row_count)]
        + [pltpu.SemaphoreType.DMA((13,)), pltpu.SemaphoreType.DMA((chunks,))]
        + [pltpu.SemaphoreType.DMA((count - 1,)) for count in (row_count, src_count, row_count)] * 2,
        compiler_params=pltpu.CompilerParams(
            collective_id=0, has_side_effects=True, vmem_limit_bytes=60 * 1024 * 1024
        ),
    )(*scalars, *arrays)


def solution(mesh):
    placed = (P("rows", None), P("rows", "src"), P(), P(), P())
    return jax.shard_map(
        local, mesh=mesh, in_specs=placed, out_specs=P("rows", "src"), check_vma=False
    )
```
